32 devices in a mesh: row: 4 (over y, core), col: 8 (over z, x).
Axes of the slice: x: 2, y: 2, z: 4, core: 2. Of those that a mesh axis runs over, the one named last changes fastest.
Arguments:
- node_feats: bfloat16 [4096, 128], P(('row', 'col')), may hold values from -6 to 6
- send_rows: int32 [4, 8, 8, 32], P('row', 'col'), may hold values from 0 to 127
- send_count: int32 [4, 8, 8], P('row', 'col'), may hold values from 8 to 32, as said below
- block_tiles: int32 [4, 8, 4, 5], P('row', 'col'), may hold values from 0 to 1
- block_values: bfloat16 [4, 8, 4, 5, 128, 128], P('row', 'col'), may hold values from 0 to 1, as said below
- w_self: bfloat16 [128, 256], replicated, may hold values from -0.5 to 0.5
- w_neigh: bfloat16 [128, 256], replicated, may hold values from -1 to 1
- bias_term: float32 [256], replicated, may hold values from -3 to 3
- cotangent: bfloat16 [4096, 256], P(('row', 'col')), may hold values from -6 to 6
Outputs:
- hidden: bfloat16 [4096, 256], P(('row', 'col'))
- input_grads: float32 [4096, 128], P(('row', 'col'))
- self_grads: float32 [128, 256], replicated
- neigh_grads: float32 [128, 256], replicated
- bias_grads: float32 [256], replicated
The draws below stay inside these ranges and needn't reach their ends.
Inputs may be any that keep to these rules, and one draw needn't show every extreme that they name: `send_rows`: slots at or past a list's count carry no data. `send_count`: every sending device fills all 32 slots toward at least one peer. `block_values`: each entry is 0 or 1.
All inputs are finite; a program needn't handle non-finite values.
Results may differ from the reference program's by a relative error of at most 0.0055.
Values may be sent and summed in bfloat16 or wider, within the bound.
A program may use at most 64 MiB of HBM per device.

```python
import jax
import jax.numpy as jnp
from jax import lax

FIN = 128
HID = 256
ND = 128
BND = 32
KT = 5
PANEL = 512
TILES = 2
NODES = 4096
N_ROW = 4
N_COL = 8


def draw_send_count(key, part):
    key = jax.random.fold_in(key, 3)
    key_base, key_full = jax.random.split(key)
    shape = (N_ROW, N_COL, N_COL)
    base = jax.random.randint(key_base, shape, BND // 4, BND + 1)
    full_peer = jax.random.randint(key_full, (N_ROW, N_COL, 1), 0, N_COL)
    peers = lax.broadcasted_iota(jnp.int32, shape, 2)
    return jnp.where(peers == full_peer, BND, base).astype(jnp.int32)


def draw_block_values(key, part):
    key = jax.random.fold_in(key, 7)
    key_rate, key_keep, key_edge = jax.random.split(key, 3)
    rate_shape = (1, N_COL, PANEL // 128, 1, 128, 1)
    log_rate = jax.random.uniform(key_rate, rate_shape, jnp.float32, -4.0, -1.0)
    keeping = jax.random.uniform(key_keep, rate_shape, jnp.float32) > 0.0625
    density = jnp.exp(log_rate) * keeping.astype(jnp.float32)
    shape = (N_ROW, N_COL, PANEL // 128, KT, 128, 128)
    edges = jax.random.uniform(key_edge, shape, jnp.float32) < density
    return edges.astype(jnp.float32).astype(jnp.bfloat16)


def set_ends(result, stream_key, least, top_value):
    index_at = [jax.random.randint(jax.random.fold_in(stream_key, axis), (), 0, length) for axis, length in enumerate(result.shape)]
    longest = result.shape.index(max(result.shape))
    next_to = index_at[:longest] + [(index_at[longest] + 1) % result.shape[longest]] + index_at[longest + 1:]
    return result.at[tuple(index_at)].set(least).at[tuple(next_to)].set(top_value)


def level_of(own_key, shape, cuts, least, high):
    gain = 1.0
    for dim, shards_of in cuts:
        steps = jax.random.uniform(jax.random.fold_in(jax.random.fold_in(own_key, 6), dim), (shards_of,), jnp.float32, least / len(cuts), high / len(cuts))
        gain = gain * jnp.repeat(jnp.exp(steps), shape[dim] // shards_of).reshape((-1,) + (1,) * (len(shape) - 1 - dim))
    return gain


def centred(own_key, shape, width, reach, cuts=(), kind=jnp.bfloat16):
    array = width * jax.random.normal(own_key, shape, jnp.float32)
    if cuts:
        array = array * level_of(own_key, shape, cuts, -0.22, 0.18)
    return jnp.clip(array, -reach, reach).astype(kind)


def setup_inputs(seed: int = 0) -> dict:
    key_of = jax.random.split(jax.random.key(seed), 10)
    node_feats = centred(key_of[0], (NODES, FIN), 1.0, 6.0, ((0, 32),))
    send_rows = set_ends(jax.random.randint(key_of[1], (N_ROW, N_COL, N_COL, BND), 0, ND), jax.random.fold_in(key_of[1], 1), 0, ND - 1).astype(jnp.int32)
    send_count = draw_send_count(jax.random.fold_in(key_of[9], 71), 0)
    block_tiles = set_ends(jax.random.randint(key_of[3], (N_ROW, N_COL, PANEL // 128, KT), 0, TILES), jax.random.fold_in(key_of[3], 1), 0, TILES - 1).astype(jnp.int32)
    block_values = draw_block_values(jax.random.fold_in(key_of[9], 71), 0)
    w_self = centred(key_of[5], (FIN, HID), FIN ** -0.5, 0.5)
    w_neigh = centred(key_of[6], (FIN, HID), (FIN // 4) ** -0.5, 1.0)
    bias_term = centred(key_of[7], (HID,), 0.5, 3.0, (), jnp.float32)
    cotangent = centred(key_of[8], (NODES, HID), 1.0, 6.0, ((0, 32),))
    return dict(node_feats=node_feats, send_rows=send_rows, send_count=send_count, block_tiles=block_tiles, block_values=block_values, w_self=w_self, w_neigh=w_neigh, bias_term=bias_term, cotangent=cotangent)


def take_rows(local_rows, indices):
    return local_rows[indices]


def scatter_rows(indices, contrib):
    zeros = jnp.zeros((ND, FIN), jnp.float32)
    return zeros.at[indices.reshape(-1)].add(contrib.reshape(-1, FIN))


def aggregate(inputs):
    tile_rows, indices, values = inputs
    picked = tile_rows[indices].astype(jnp.float32)
    partial_value = jnp.einsum('pkij,pkjf->pif', values.astype(jnp.float32), picked)
    return partial_value.reshape(PANEL, FIN)


def reference(node_feats, send_rows, send_count, block_tiles, block_values, w_self, w_neigh, bias_term, cotangent):
    local = node_feats.reshape(N_ROW, N_COL, ND, FIN)
    slots = lax.broadcasted_iota(jnp.int32, (N_ROW, N_COL, N_COL, BND), 3)
    live_slots = slots < send_count[..., None]
    chosen = jax.vmap(jax.vmap(take_rows))(local, send_rows)
    outgoing = jnp.where(live_slots[..., None], chosen, 0.0).astype(jnp.bfloat16)
    incoming = jnp.swapaxes(outgoing, 1, 2).reshape(N_ROW, N_COL, TILES, 128, FIN)

    def forward_row(carry, inputs):
        return carry + lax.map(aggregate, inputs), None

    start = jnp.zeros((N_COL, PANEL, FIN), jnp.float32)
    panel_sums, unused = lax.scan(forward_row, start, (incoming, block_tiles, block_values))
    degree = jnp.sum(block_values, axis=(0, 3, 5), dtype=jnp.float32).reshape(N_COL, N_ROW, ND)
    degree = jnp.swapaxes(degree, 0, 1).reshape(-1)
    agg_sum = jnp.swapaxes(panel_sums.reshape(N_COL, N_ROW, ND, FIN), 0, 1).reshape(-1, FIN)
    divisor = jnp.maximum(degree, 1.0)
    neigh_mean = (agg_sum / divisor[:, None]).astype(jnp.bfloat16)
    preact = (jnp.dot(node_feats, w_self, preferred_element_type=jnp.float32)
              + jnp.dot(neigh_mean, w_neigh, preferred_element_type=jnp.float32) + bias_term)
    hidden = jax.nn.silu(preact).astype(jnp.bfloat16)
    sigmoid_pre = jax.nn.sigmoid(preact)
    pre_grads = (cotangent.astype(jnp.float32) * sigmoid_pre * (1.0 + preact * (1.0 - sigmoid_pre))).astype(jnp.bfloat16)
    self_grads = jnp.dot(node_feats.T, pre_grads, preferred_element_type=jnp.float32)
    neigh_grads = jnp.dot(neigh_mean.T, pre_grads, preferred_element_type=jnp.float32)
    bias_grads = jnp.sum(pre_grads.astype(jnp.float32), axis=0)
    mean_grads = (jnp.dot(pre_grads, w_neigh.T, preferred_element_type=jnp.float32) / divisor[:, None]).astype(jnp.bfloat16)
    panels = jnp.swapaxes(mean_grads.reshape(N_ROW, N_COL, ND, FIN), 0, 1).reshape(N_COL, PANEL, FIN)

    def spread(inputs):
        blocks, indices, values = inputs
        source = blocks.reshape(PANEL // 128, 128, FIN).astype(jnp.float32)
        spread_back = jnp.einsum('pkij,pif->pkjf', values.astype(jnp.float32), source)
        summed = jax.ops.segment_sum(spread_back.reshape(-1, 128, FIN), indices.reshape(-1), num_segments=TILES)
        return summed.reshape(N_COL, BND, FIN)

    def backward_row(inputs):
        indices, values, rows_list, live_row = inputs
        tile_grads = lax.map(spread, (panels, indices, values))
        returned = jnp.swapaxes(tile_grads, 0, 1)
        masked = jnp.where(live_row[..., None], returned, 0.0)
        return jax.vmap(scatter_rows)(rows_list, masked)

    collected = lax.map(backward_row, (block_tiles, block_values, send_rows, live_slots))
    input_grads = collected.reshape(-1, FIN) + jnp.dot(pre_grads, w_self.T, preferred_element_type=jnp.float32)
    return hidden, input_grads, self_grads, neigh_grads, bias_grads
```

```python
import functools

import jax
import jax.numpy as jnp
from jax import lax
from jax.experimental import pallas as pl
from jax.experimental.pallas import tpu as pltpu
from jax.sharding import PartitionSpec as P

BF = jnp.bfloat16
F32 = jnp.float32
MESH = pl.DeviceIdType.MESH
PIECE = 16


def mm(left, right, contract=(1, 0)):
    return lax.dot_general(
        left, right, (((contract[0],), (contract[1],)), ((), ())), preferred_element_type=F32
    )


def each(first, count, body):
    if count - first <= 8:
        for step in range(first, count):
            body(step)
    else:
        lax.fori_loop(first, count, lambda step, carry: (body(step), carry)[1], 0)


def rows_at(ref, index, size):
    if not isinstance(index, int):
        return ref.at[pl.ds(pl.multiple_of(index * size, size), size)]
    return ref.at[pl.ds(index * size, size)]


def layer_kernel(
    row_count, col_count,
    feats_h, rows_h, count_h, tiles_h, values_h, w_self_h, w_neigh_h, bias_h, cot_h,
    hidden_o, base_o, grads_o, bias_o,
    feats, rows, count, tiles, values, w_self, w_neigh, bias, cot,
    onehot, outgoing, inbox, weights, weights_t, deg_out, deg_in, part_out, part_in,
    panel, grad_out, grad_in, bias_row, bias_in, bias_col, bias_in2, back_out, back_in,
    piece_out, piece_in,
    load_sem, send_a, recv_a, send_d, recv_d, send_p, recv_p, send_m, recv_m, send_g, recv_g,
    send_b, recv_b, send_t, recv_t, send_c, recv_c, send_h, recv_h, send_x, recv_x, send_y, recv_y,
):
    node_count, in_width = feats.shape
    slot_count = rows.shape[3]
    tile_count = inbox.shape[0] // 128
    depth = tiles.shape[3]
    grad_rows = grads_o.shape[0]
    share = grad_rows // row_count
    piece = max(PIECE, share // col_count)
    owners = share // piece
    r = lax.axis_index("row")
    c = lax.axis_index("col")

    def row_peer(step):
        return lax.rem(r + step, row_count)

    def col_peer(step):
        return lax.rem(c + step, col_count)

    def row_source(step):
        return lax.rem(r + row_count - step, row_count)

    def col_source(step):
        return lax.rem(c + col_count - step, col_count)

    loads = []
    pairs = (
        (rows_h, rows), (count_h, count), (feats_h, feats), (tiles_h, tiles), (values_h, values),
        (w_self_h, w_self), (w_neigh_h, w_neigh), (bias_h, bias), (cot_h, cot),
    )
    for number, (source, target) in enumerate(pairs):
        copy = pltpu.make_async_copy(source, target, load_sem.at[number])
        copy.start()
        loads.append(copy)

    barrier = pltpu.get_barrier_semaphore()
    each(1, row_count, lambda s: pl.semaphore_signal(
        barrier, inc=1, device_id=(row_peer(s), c), device_id_type=MESH))
    each(1, col_count, lambda s: pl.semaphore_signal(
        barrier, inc=1, device_id=(r, col_peer(s)), device_id_type=MESH))

    def remote(source, target, send, recv, device):
        return pltpu.make_async_remote_copy(
            src_ref=source, dst_ref=target, send_sem=send, recv_sem=recv,
            device_id=device, device_id_type=MESH)

    def to_row(step, source, target, send, recv):
        return remote(source, target, send.at[step], recv.at[step], (row_peer(step), c))

    def to_col(step, source, target, send, recv):
        return remote(source, target, send.at[step], recv.at[step], (r, col_peer(step)))

    for copy in loads[:3]:
        copy.wait()
    slot = lax.broadcasted_iota(jnp.int32, (1, slot_count), 1)
    node = lax.broadcasted_iota(jnp.int32, (node_count, slot_count), 0)
    for peer in range(col_count):
        listed = jnp.where(slot < count[0, 0, peer], rows[0, 0, pl.ds(peer, 1), :], -1)
        hot = (node == listed).astype(F32).astype(BF)
        onehot[:, pl.ds(peer * slot_count, slot_count)] = hot
    outgoing[...] = mm(onehot[...], feats[...], (0, 0)).astype(BF)

    pl.semaphore_wait(barrier, row_count + col_count - 2)

    def feature_copy(step):
        return to_col(step, rows_at(outgoing, col_peer(step), slot_count),
                      rows_at(inbox, c, slot_count), send_a, recv_a)

    each(1, col_count, lambda s: feature_copy(s).start())
    rows_at(inbox, c, slot_count)[...] = rows_at(outgoing, c, slot_count)[...]

    loads[3].wait()
    loads[4].wait()
    ones = jnp.ones((8, inbox.shape[0]), BF)

    def merge(block):
        for tile in range(tile_count):
            total = jnp.zeros((128, 128), F32)
            for k in range(depth):
                chosen = (tiles[0, 0, block, k] == tile).astype(F32)
                total += values[0, 0, block, k].astype(F32) * chosen
            merged = total.astype(BF)
            rows_at(weights, block, 128)[:, pl.ds(tile * 128, 128)] = merged
        deg_out[block] = mm(ones, rows_at(weights, block, 128)[...], (1, 1))

    each(0, row_count, merge)

    def degree_copy(step):
        return to_row(step, deg_out.at[row_peer(step)], deg_in.at[r], send_d, recv_d)

    each(1, row_count, lambda s: degree_copy(s).start())
    deg_in[r] = deg_out[r]

    def turn(block):
        start = block * 128 if isinstance(block, int) else pl.multiple_of(block * 128, 128)
        weights_t[:, pl.ds(start, 128)] = rows_at(weights, block, 128)[...].astype(F32).T.astype(BF)

    each(0, row_count, turn)
    for copy in loads[5:]:
        copy.wait()
    own_part = mm(feats[...], w_self[...]) + bias[...]
    each(1, row_count, lambda s: degree_copy(s).wait_recv())
    degree = deg_in[0]
    for other in range(1, row_count):
        degree = degree + deg_in[other]
    inverse = 1.0 / jnp.maximum(degree[0:1, :], 1.0)
    inverse = jnp.broadcast_to(inverse, (128, 128)).T

    each(1, col_count, lambda s: feature_copy(s).wait_recv())

    def partial_copy(step):
        return to_row(step, rows_at(part_out, row_peer(step), 128), part_in.at[r], send_p, recv_p)

    def aggregate(step):
        block = row_peer(step)
        rows_at(part_out, block, 128)[...] = mm(
            rows_at(weights, block, 128)[...], inbox[...]).astype(BF)
        partial_copy(step).start()

    each(1, row_count, aggregate)
    agg_sum = mm(rows_at(weights, r, 128)[...], inbox[...])
    part_in[r] = jnp.zeros((128, in_width), BF)
    each(1, row_count, lambda s: partial_copy(s).wait_recv())
    for other in range(row_count):
        agg_sum = agg_sum + part_in[other].astype(F32)

    neigh_mean = (agg_sum * inverse).astype(BF)
    preact = own_part + mm(neigh_mean, w_neigh[...])
    sigmoid_pre = jax.nn.sigmoid(preact)
    pre_grads = (
        cot[...].astype(F32) * sigmoid_pre * (1.0 + preact * (1.0 - sigmoid_pre))
    ).astype(BF)
    rows_at(panel, r, 128)[...] = (mm(pre_grads, w_neigh[...], (1, 1)) * inverse).astype(BF)

    def panel_copy(step):
        return to_row(step, rows_at(panel, r, 128), rows_at(panel, r, 128), send_m, recv_m)

    each(1, row_count, lambda s: panel_copy(s).start())

    half = grad_out.shape[1]
    for number, left in enumerate((feats[...], neigh_mean)):
        product = mm(left, pre_grads, (0, 0)).astype(BF)
        for side in range(2):
            grad_out[pl.ds((2 * number + side) * in_width, in_width), :] = (
                product[:, side * half:(side + 1) * half])

    def share_copy(step):
        return to_row(step, rows_at(grad_out, row_peer(step), share), grad_in.at[r], send_g, recv_g)

    each(1, row_count, lambda s: share_copy(s).start())
    grad_in[r] = rows_at(grad_out, r, share)[...]
    bias_row[...] = mm(jnp.ones((8, node_count), BF), pre_grads)

    def bias_copy(step):
        return to_row(step, bias_row, bias_in.at[r], send_b, recv_b)

    each(1, row_count, lambda s: bias_copy(s).start())
    bias_in[r] = bias_row[...]
    hidden_o[...] = (preact * sigmoid_pre).astype(BF)
    base = mm(pre_grads, w_self[...], (1, 1))

    each(1, row_count, lambda s: panel_copy(s).wait_recv())
    back_out[...] = mm(weights_t[...], panel[...]).astype(BF)

    def back_copy(step):
        return to_col(step, rows_at(back_out, col_peer(step), slot_count),
                      rows_at(back_in, c, slot_count), send_t, recv_t)

    each(1, col_count, lambda s: back_copy(s).start())
    rows_at(back_in, c, slot_count)[...] = rows_at(back_out, c, slot_count)[...]

    def owning(holder, body):
        if owners == col_count:
            body()
        else:
            pl.when(holder < owners)(body)

    def piece_copy(step):
        return to_col(step, rows_at(piece_out, col_peer(step) % owners, piece),
                      piece_in.at[c], send_c, recv_c)

    each(1, row_count, lambda s: share_copy(s).wait_recv())
    total = grad_in[0].astype(F32)
    for other in range(1, row_count):
        total = total + grad_in[other].astype(F32)
    piece_out[...] = total.astype(BF)
    each(1, col_count, lambda s: owning(col_peer(s), lambda: piece_copy(s).start()))
    piece_in[c] = rows_at(piece_out, c % owners, piece)[...]

    each(1, row_count, lambda s: bias_copy(s).wait_recv())
    bias_total = bias_in[0]
    for other in range(1, row_count):
        bias_total = bias_total + bias_in[other]
    bias_col[...] = bias_total

    def bias_copy2(step):
        return to_col(step, bias_col, bias_in2.at[c], send_h, recv_h)

    each(1, col_count, lambda s: bias_copy2(s).start())
    bias_in2[c] = bias_col[...]

    def final_piece(holder):
        start = r * share + holder * piece
        return grads_o.at[pl.ds(pl.multiple_of(start, piece), piece)]

    def final_copy(step):
        return to_col(step, final_piece(c), final_piece(c), send_x, recv_x)

    def reduce_piece():
        each(1, col_count, lambda s: piece_copy(s).wait_recv())
        whole = piece_in[0].astype(F32)
        for other in range(1, col_count):
            whole = whole + piece_in[other].astype(F32)
        final_piece(c)[...] = whole.astype(BF)
        each(1, col_count, lambda s: final_copy(s).start())

    owning(c, reduce_piece)

    each(1, col_count, lambda s: back_copy(s).wait_recv())
    base_o[...] = base + mm(onehot[...], back_in[...])
    each(1, col_count, lambda s: bias_copy2(s).wait_recv())
    bias_total = bias_in2[0]
    for other in range(1, col_count):
        bias_total = bias_total + bias_in2[other]
    bias_o[...] = bias_total

    each(1, col_count, lambda s: owning(col_source(s), lambda: final_copy(s).wait_recv()))

    def share_final(step):
        own = rows_at(grads_o, r, share)
        return to_row(step, own, own, send_y, recv_y)

    each(1, row_count, lambda s: share_final(s).start())
    each(1, row_count, lambda s: share_final(s).wait_recv())

    for step_copy in (degree_copy, partial_copy, panel_copy, share_copy, bias_copy, share_final):
        each(1, row_count, lambda s: step_copy(s).wait_send())
    for step_copy in (feature_copy, back_copy, bias_copy2):
        each(1, col_count, lambda s: step_copy(s).wait_send())
    each(1, col_count, lambda s: owning(col_peer(s), lambda: piece_copy(s).wait_send()))
    owning(c, lambda: each(1, col_count, lambda s: final_copy(s).wait_send()))


def write_kernel(hidden_i, base_i, grads_i, bias_i, hidden, base, self_grads, neigh_grads, bias):
    hidden[...] = hidden_i[...]
    base[...] = base_i[...]
    rows, width = self_grads.shape
    half = grads_i.shape[1]
    for number, target in enumerate((self_grads, neigh_grads)):
        for side in range(width // half):
            block = grads_i[pl.ds((2 * number + side) * rows, rows), :]
            target[:, pl.ds(side * half, half)] = block.astype(F32)
    bias[...] = bias_i[0:1, :]


def shards(row_count, col_count, node_feats, send_rows, send_count, block_tiles, block_values,
           w_self, w_neigh, bias_term, cotangent):
    nodes, width = node_feats.shape
    hid = w_self.shape[1]
    half = hid // 2
    slots = send_rows.shape[3]
    received = col_count * slots
    panel = row_count * nodes
    grad_rows = 4 * width
    share = grad_rows // row_count
    piece = max(PIECE, share // col_count)
    bias_term = bias_term.reshape(1, hid)
    arrays = (node_feats, send_rows, send_count, block_tiles, block_values, w_self, w_neigh,
              bias_term, cotangent)
    spaces = (pltpu.VMEM, pltpu.VMEM, pltpu.SMEM, pltpu.SMEM) + (pltpu.VMEM,) * 5
    row_sems = pltpu.SemaphoreType.DMA((row_count,))
    col_sems = pltpu.SemaphoreType.DMA((col_count,))
    vmem = pl.BlockSpec(memory_space=pltpu.VMEM)
    scratch = [space(array.shape, array.dtype) for space, array in zip(spaces, arrays)] + [
        pltpu.VMEM((nodes, received), BF),
        pltpu.VMEM((received, width), BF),
        pltpu.VMEM((received, width), BF),
        pltpu.VMEM((panel, received), BF),
        pltpu.VMEM((received, panel), BF),
        pltpu.VMEM((row_count, 8, nodes), F32),
        pltpu.VMEM((row_count, 8, nodes), F32),
        pltpu.VMEM((panel, width), BF),
        pltpu.VMEM((row_count, nodes, width), BF),
        pltpu.VMEM((panel, width), BF),
        pltpu.VMEM((grad_rows, half), BF),
        pltpu.VMEM((row_count, share, half), BF),
        pltpu.VMEM((8, hid), F32),
        pltpu.VMEM((row_count, 8, hid), F32),
        pltpu.VMEM((8, hid), F32),
        pltpu.VMEM((col_count, 8, hid), F32),
        pltpu.VMEM((received, width), BF),
        pltpu.VMEM((received, width), BF),
        pltpu.VMEM((share, half), BF),
        pltpu.VMEM((col_count, piece, half), BF),
        pltpu.SemaphoreType.DMA((len(arrays),)),
        col_sems, col_sems, row_sems, row_sems, row_sems, row_sems, row_sems, row_sems,
        row_sems, row_sems, row_sems, row_sems, col_sems, col_sems, col_sems, col_sems,
        col_sems, col_sems, col_sems, col_sems, row_sems, row_sems,
    ]
    results = pl.pallas_call(
        functools.partial(layer_kernel, row_count, col_count),
        out_shape=(
            jax.ShapeDtypeStruct((nodes, hid), BF),
            jax.ShapeDtypeStruct((nodes, width), F32),
            jax.ShapeDtypeStruct((grad_rows, half), BF),
            jax.ShapeDtypeStruct((8, hid), F32),
        ),
        in_specs=[pl.BlockSpec(memory_space=pl.ANY)] * len(arrays),
        out_specs=(vmem,) * 4,
        scratch_shapes=scratch,
        compiler_params=pltpu.CompilerParams(
            collective_id=0, has_side_effects=True, vmem_limit_bytes=40 * 1024 * 1024),
    )(*arrays)
    hidden, input_grads, self_grads, neigh_grads, bias_grads = pl.pallas_call(
        write_kernel,
        out_shape=(
            jax.ShapeDtypeStruct((nodes, hid), BF),
            jax.ShapeDtypeStruct((nodes, width), F32),
            jax.ShapeDtypeStruct((width, hid), F32),
            jax.ShapeDtypeStruct((width, hid), F32),
            jax.ShapeDtypeStruct((1, hid), F32),
        ),
        in_specs=[vmem] * 4,
        out_specs=(vmem,) * 5,
    )(*results)
    return hidden, input_grads, self_grads, neigh_grads, bias_grads.reshape(hid)


def solution(mesh):
    placed = (
        P(("row", "col"), None),
        P("row", "col", None, None),
        P("row", "col", None),
        P("row", "col", None, None),
        P("row", "col", None, None, None, None),
        P(),
        P(),
        P(),
        P(("row", "col"), None),
    )
    return jax.shard_map(
        functools.partial(shards, mesh.shape["row"], mesh.shape["col"]),
        mesh=mesh,
        in_specs=placed,
        out_specs=(P(("row", "col"), None), P(("row", "col"), None), P(), P(), P()),
        check_vma=False,
    )
```

```python
import functools

import jax
import jax.numpy as jnp
from jax import lax
from jax.experimental import pallas as pl
from jax.experimental.pallas import tpu as pltpu
from jax.sharding import PartitionSpec as P

BF = jnp.bfloat16
F32 = jnp.float32
MESH = pl.DeviceIdType.MESH
PIECE = 16


def mm(left, right, contract=(1, 0)):
    return lax.dot_general(
        left, right, (((contract[0],), (contract[1],)), ((), ())), preferred_element_type=F32
    )


def each(first, count, body):
    if count - first <= 32:
        for step in range(first, count):
            body(step)
    else:
        lax.fori_loop(first, count, lambda step, carry: (body(step), carry)[1], 0)


def rows_at(ref, index, size):
    if not isinstance(index, int):
        return ref.at[pl.ds(pl.multiple_of(index * size, size), size)]
    return ref.at[pl.ds(index * size, size)]


def layer_kernel(
    row_count, col_count,
    feats_h, rows_h, count_h, tiles_h, values_h, w_self_h, w_neigh_h, bias_h, cot_h,
    hidden_o, base_o, grads_o, bias_o,
    feats, rows, count, tiles, values, w_self, w_neigh, bias, cot,
    onehot, outgoing, inbox, weights, weights_t, deg_out, deg_in, part_out, part_in,
    panel, grad_out, grad_in, bias_row, bias_in, bias_col, bias_in2, back_out, back_in,
    piece_out, piece_in,
    load_sem, send_a, recv_a, send_d, recv_d, send_p, recv_p, send_m, recv_m, send_g, recv_g,
    send_b, recv_b, send_t, recv_t, send_c, recv_c, send_h, recv_h, send_x, recv_x, send_y, recv_y, send_z, recv_z,
):
    node_count, in_width = feats.shape
    slot_count = rows.shape[3]
    tile_count = inbox.shape[0] // 128
    depth = tiles.shape[3]
    grad_rows = grads_o.shape[0]
    share = grad_rows // row_count
    piece = max(PIECE, share // col_count)
    owners = share // piece
    total_count = row_count * col_count
    direct = total_count * PIECE == grad_rows
    r = lax.axis_index("row")
    c = lax.axis_index("col")

    def row_peer(step):
        return lax.rem(r + step, row_count)

    def col_peer(step):
        return lax.rem(c + step, col_count)

    me = r * col_count + c

    def any_peer(step):
        return lax.rem(me + step, total_count)

    def place_of(index):
        return (index // col_count, lax.rem(index, col_count))

    def col_source(step):
        return lax.rem(c + col_count - step, col_count)

    loads = []
    pairs = (
        (rows_h, rows), (count_h, count), (feats_h, feats), (tiles_h, tiles), (values_h, values),
        (w_self_h, w_self), (w_neigh_h, w_neigh), (bias_h, bias), (cot_h, cot),
    )
    for number, (source, target) in enumerate(pairs):
        copy = pltpu.make_async_copy(source, target, load_sem.at[number])
        copy.start()
        loads.append(copy)

    barrier = pltpu.get_barrier_semaphore()
    if direct:
        each(1, total_count, lambda s: pl.semaphore_signal(
            barrier, inc=1, device_id=place_of(any_peer(s)), device_id_type=MESH))
    else:
        each(1, row_count, lambda s: pl.semaphore_signal(
            barrier, inc=1, device_id=(row_peer(s), c), device_id_type=MESH))
        each(1, col_count, lambda s: pl.semaphore_signal(
            barrier, inc=1, device_id=(r, col_peer(s)), device_id_type=MESH))
    greeted = total_count - 1 if direct else row_count + col_count - 2

    def remote(source, target, send, recv, device):
        return pltpu.make_async_remote_copy(
            src_ref=source, dst_ref=target, send_sem=send, recv_sem=recv,
            device_id=device, device_id_type=MESH)

    def to_row(step, source, target, send, recv):
        return remote(source, target, send.at[step], recv.at[step], (row_peer(step), c))

    def to_col(step, source, target, send, recv):
        return remote(source, target, send.at[step], recv.at[step], (r, col_peer(step)))

    for copy in loads[:3]:
        copy.wait()
    slot = lax.broadcasted_iota(jnp.int32, (1, slot_count), 1)
    node = lax.broadcasted_iota(jnp.int32, (node_count, slot_count), 0)
    for peer in range(col_count):
        listed = jnp.where(slot < count[0, 0, peer], rows[0, 0, pl.ds(peer, 1), :], -1)
        hot = (node == listed).astype(F32).astype(BF)
        onehot[:, pl.ds(peer * slot_count, slot_count)] = hot
    outgoing[...] = mm(onehot[...], feats[...], (0, 0)).astype(BF)

    pl.semaphore_wait(barrier, greeted)

    def feature_copy(step):
        return to_col(step, rows_at(outgoing, col_peer(step), slot_count),
                      rows_at(inbox, c, slot_count), send_a, recv_a)

    each(1, col_count, lambda s: feature_copy(s).start())
    rows_at(inbox, c, slot_count)[...] = rows_at(outgoing, c, slot_count)[...]

    loads[3].wait()
    loads[4].wait()
    ones = jnp.ones((8, inbox.shape[0]), BF)

    def merge(block):
        for tile in range(tile_count):
            total = jnp.zeros((128, 128), F32)
            for k in range(depth):
                chosen = (tiles[0, 0, block, k] == tile).astype(F32)
                total += values[0, 0, block, k].astype(F32) * chosen
            merged = total.astype(BF)
            rows_at(weights, block, 128)[:, pl.ds(tile * 128, 128)] = merged
        deg_out[block] = mm(ones, rows_at(weights, block, 128)[...], (1, 1))

    each(0, row_count, merge)

    def degree_copy(step):
        return to_row(step, deg_out.at[row_peer(step)], deg_in.at[r], send_d, recv_d)

    each(1, row_count, lambda s: degree_copy(s).start())
    deg_in[r] = deg_out[r]

    def turn(block):
        start = block * 128 if isinstance(block, int) else pl.multiple_of(block * 128, 128)
        weights_t[:, pl.ds(start, 128)] = rows_at(weights, block, 128)[...].astype(F32).T.astype(BF)

    each(0, row_count, turn)
    for copy in loads[5:]:
        copy.wait()
    own_part = mm(feats[...], w_self[...]) + bias[...]
    each(1, row_count, lambda s: degree_copy(s).wait_recv())
    degree = deg_in[0]
    for other in range(1, row_count):
        degree = degree + deg_in[other]
    inverse = 1.0 / jnp.maximum(degree[0:1, :], 1.0)
    inverse = jnp.broadcast_to(inverse, (128, 128)).T

    each(1, col_count, lambda s: feature_copy(s).wait_recv())

    def partial_copy(step):
        return to_row(step, rows_at(part_out, row_peer(step), 128), part_in.at[r], send_p, recv_p)

    def aggregate(step):
        block = row_peer(step)
        rows_at(part_out, block, 128)[...] = mm(
            rows_at(weights, block, 128)[...], inbox[...]).astype(BF)
        partial_copy(step).start()

    each(1, row_count, aggregate)
    agg_sum = mm(rows_at(weights, r, 128)[...], inbox[...])
    part_in[r] = jnp.zeros((128, in_width), BF)
    each(1, row_count, lambda s: partial_copy(s).wait_recv())
    for other in range(row_count):
        agg_sum = agg_sum + part_in[other].astype(F32)

    neigh_mean = (agg_sum * inverse).astype(BF)
    preact = own_part + mm(neigh_mean, w_neigh[...])
    sigmoid_pre = jax.nn.sigmoid(preact)
    pre_grads = (
        cot[...].astype(F32) * sigmoid_pre * (1.0 + preact * (1.0 - sigmoid_pre))
    ).astype(BF)
    rows_at(panel, r, 128)[...] = (mm(pre_grads, w_neigh[...], (1, 1)) * inverse).astype(BF)

    def panel_copy(step):
        return to_row(step, rows_at(panel, r, 128), rows_at(panel, r, 128), send_m, recv_m)

    each(1, row_count, lambda s: panel_copy(s).start())

    half = grad_out.shape[1]
    for number, left in enumerate((feats[...], neigh_mean)):
        product = mm(left, pre_grads, (0, 0)).astype(BF)
        for side in range(2):
            grad_out[pl.ds((2 * number + side) * in_width, in_width), :] = (
                product[:, side * half:(side + 1) * half])

    def share_copy(step):
        return to_row(step, rows_at(grad_out, row_peer(step), share), grad_in.at[r], send_g, recv_g)

    def spread_copy(step):
        peer = any_peer(step)
        return remote(rows_at(grad_out, peer, PIECE), piece_in.at[me],
                      send_c.at[step], recv_c.at[step], place_of(peer))

    def gather_copy(step):
        own = rows_at(grads_o, me, PIECE)
        return remote(own, own, send_z.at[step], recv_z.at[step], place_of(any_peer(step)))

    if direct:
        each(1, total_count, lambda s: spread_copy(s).start())
        piece_in[me] = rows_at(grad_out, me, PIECE)[...]
    else:
        each(1, row_count, lambda s: share_copy(s).start())
        grad_in[r] = rows_at(grad_out, r, share)[...]
    bias_row[...] = mm(jnp.ones((8, node_count), BF), pre_grads)

    def bias_copy(step):
        return to_row(step, bias_row, bias_in.at[r], send_b, recv_b)

    each(1, row_count, lambda s: bias_copy(s).start())
    bias_in[r] = bias_row[...]
    hidden_o[...] = (preact * sigmoid_pre).astype(BF)
    base = mm(pre_grads, w_self[...], (1, 1))

    each(1, row_count, lambda s: panel_copy(s).wait_recv())
    back_out[...] = mm(weights_t[...], panel[...]).astype(BF)

    def back_copy(step):
        return to_col(step, rows_at(back_out, col_peer(step), slot_count),
                      rows_at(back_in, c, slot_count), send_t, recv_t)

    each(1, col_count, lambda s: back_copy(s).start())
    rows_at(back_in, c, slot_count)[...] = rows_at(back_out, c, slot_count)[...]

    def owning(holder, body):
        if owners == col_count:
            body()
        else:
            pl.when(holder < owners)(body)

    def piece_copy(step):
        return to_col(step, rows_at(piece_out, col_peer(step) % owners, piece),
                      piece_in.at[c], send_c, recv_c)

    if direct:
        each(1, total_count, lambda s: spread_copy(s).wait_recv())
        whole = piece_in[0].astype(F32)
        for other in range(1, total_count):
            whole = whole + piece_in[other].astype(F32)
        rows_at(grads_o, me, PIECE)[...] = whole.astype(BF)
        each(1, total_count, lambda s: gather_copy(s).start())
    else:
        each(1, row_count, lambda s: share_copy(s).wait_recv())
        total = grad_in[0].astype(F32)
        for other in range(1, row_count):
            total = total + grad_in[other].astype(F32)
        piece_out[...] = total.astype(BF)
        each(1, col_count, lambda s: owning(col_peer(s), lambda: piece_copy(s).start()))
        piece_in[c] = rows_at(piece_out, c % owners, piece)[...]

    each(1, row_count, lambda s: bias_copy(s).wait_recv())
    bias_total = bias_in[0]
    for other in range(1, row_count):
        bias_total = bias_total + bias_in[other]
    bias_col[...] = bias_total

    def bias_copy2(step):
        return to_col(step, bias_col, bias_in2.at[c], send_h, recv_h)

    each(1, col_count, lambda s: bias_copy2(s).start())
    bias_in2[c] = bias_col[...]

    def final_piece(holder):
        start = r * share + holder * piece
        return grads_o.at[pl.ds(pl.multiple_of(start, piece), piece)]

    def final_copy(step):
        return to_col(step, final_piece(c), final_piece(c), send_x, recv_x)

    def reduce_piece():
        each(1, col_count, lambda s: piece_copy(s).wait_recv())
        whole = piece_in[0].astype(F32)
        for other in range(1, col_count):
            whole = whole + piece_in[other].astype(F32)
        final_piece(c)[...] = whole.astype(BF)
        each(1, col_count, lambda s: final_copy(s).start())

    if not direct:
        owning(c, reduce_piece)

    each(1, col_count, lambda s: back_copy(s).wait_recv())
    base_o[...] = base + mm(onehot[...], back_in[...])
    each(1, col_count, lambda s: bias_copy2(s).wait_recv())
    bias_total = bias_in2[0]
    for other in range(1, col_count):
        bias_total = bias_total + bias_in2[other]
    bias_o[...] = bias_total

    def share_final(step):
        own = rows_at(grads_o, r, share)
        return to_row(step, own, own, send_y, recv_y)

    if direct:
        each(1, total_count, lambda s: gather_copy(s).wait_recv())
        for step_copy in (spread_copy, gather_copy):
            each(1, total_count, lambda s: step_copy(s).wait_send())
    else:
        each(1, col_count, lambda s: owning(col_source(s), lambda: final_copy(s).wait_recv()))
        each(1, row_count, lambda s: share_final(s).start())
        each(1, row_count, lambda s: share_final(s).wait_recv())
        for step_copy in (share_copy, share_final):
            each(1, row_count, lambda s: step_copy(s).wait_send())
        each(1, col_count, lambda s: owning(col_peer(s), lambda: piece_copy(s).wait_send()))
        owning(c, lambda: each(1, col_count, lambda s: final_copy(s).wait_send()))

    for step_copy in (degree_copy, partial_copy, panel_copy, bias_copy):
        each(1, row_count, lambda s: step_copy(s).wait_send())
    for step_copy in (feature_copy, back_copy, bias_copy2):
        each(1, col_count, lambda s: step_copy(s).wait_send())


def write_kernel(hidden_i, base_i, grads_i, bias_i, hidden, base, self_grads, neigh_grads, bias):
    hidden[...] = hidden_i[...]
    base[...] = base_i[...]
    rows, width = self_grads.shape
    half = grads_i.shape[1]
    for number, target in enumerate((self_grads, neigh_grads)):
        for side in range(width // half):
            block = grads_i[pl.ds((2 * number + side) * rows, rows), :]
            target[:, pl.ds(side * half, half)] = block.astype(F32)
    bias[...] = bias_i[0:1, :]


def shards(row_count, col_count, node_feats, send_rows, send_count, block_tiles, block_values,
           w_self, w_neigh, bias_term, cotangent):
    nodes, width = node_feats.shape
    hid = w_self.shape[1]
    half = hid // 2
    slots = send_rows.shape[3]
    received = col_count * slots
    panel = row_count * nodes
    grad_rows = 4 * width
    share = grad_rows // row_count
    piece = max(PIECE, share // col_count)
    total = row_count * col_count
    pieces = total if total * PIECE == grad_rows else col_count
    piece_sems = pltpu.SemaphoreType.DMA((pieces,))
    bias_term = bias_term.reshape(1, hid)
    arrays = (node_feats, send_rows, send_count, block_tiles, block_values, w_self, w_neigh,
              bias_term, cotangent)
    spaces = (pltpu.VMEM, pltpu.VMEM, pltpu.SMEM, pltpu.SMEM) + (pltpu.VMEM,) * 5
    row_sems = pltpu.SemaphoreType.DMA((row_count,))
    col_sems = pltpu.SemaphoreType.DMA((col_count,))
    vmem = pl.BlockSpec(memory_space=pltpu.VMEM)
    scratch = [space(array.shape, array.dtype) for space, array in zip(spaces, arrays)] + [
        pltpu.VMEM((nodes, received), BF),
        pltpu.VMEM((received, width), BF),
        pltpu.VMEM((received, width), BF),
        pltpu.VMEM((panel, received), BF),
        pltpu.VMEM((received, panel), BF),
        pltpu.VMEM((row_count, 8, nodes), F32),
        pltpu.VMEM((row_count, 8, nodes), F32),
        pltpu.VMEM((panel, width), BF),
        pltpu.VMEM((row_count, nodes, width), BF),
        pltpu.VMEM((panel, width), BF),
        pltpu.VMEM((grad_rows, half), BF),
        pltpu.VMEM((row_count, share, half), BF),
        pltpu.VMEM((8, hid), F32),
        pltpu.VMEM((row_count, 8, hid), F32),
        pltpu.VMEM((8, hid), F32),
        pltpu.VMEM((col_count, 8, hid), F32),
        pltpu.VMEM((received, width), BF),
        pltpu.VMEM((received, width), BF),
        pltpu.VMEM((share, half), BF),
        pltpu.VMEM((pieces, piece, half), BF),
        pltpu.SemaphoreType.DMA((len(arrays),)),
        col_sems, col_sems, row_sems, row_sems, row_sems, row_sems, row_sems, row_sems,
        row_sems, row_sems, row_sems, row_sems, col_sems, col_sems, piece_sems, piece_sems,
        col_sems, col_sems, col_sems, col_sems, row_sems, row_sems, piece_sems, piece_sems,
    ]
    results = pl.pallas_call(
        functools.partial(layer_kernel, row_count, col_count),
        out_shape=(
            jax.ShapeDtypeStruct((nodes, hid), BF),
            jax.ShapeDtypeStruct((nodes, width), F32),
            jax.ShapeDtypeStruct((grad_rows, half), BF),
            jax.ShapeDtypeStruct((8, hid), F32),
        ),
        in_specs=[pl.BlockSpec(memory_space=pltpu.HBM)] * len(arrays),
        out_specs=(vmem,) * 4,
        scratch_shapes=scratch,
        compiler_params=pltpu.CompilerParams(
            collective_id=0, has_side_effects=True, vmem_limit_bytes=40 * 1024 * 1024),
    )(*[pltpu.with_memory_space_constraint(a, pltpu.HBM) for a in arrays])
    hidden, input_grads, self_grads, neigh_grads, bias_grads = pl.pallas_call(
        write_kernel,
        out_shape=(
            jax.ShapeDtypeStruct((nodes, hid), BF),
            jax.ShapeDtypeStruct((nodes, width), F32),
            jax.ShapeDtypeStruct((width, hid), F32),
            jax.ShapeDtypeStruct((width, hid), F32),
            jax.ShapeDtypeStruct((1, hid), F32),
        ),
        in_specs=[vmem] * 4,
        out_specs=(vmem,) * 5,
        compiler_params=pltpu.CompilerParams(vmem_limit_bytes=4 * 1024 * 1024),
    )(*results)
    return hidden, input_grads, self_grads, neigh_grads, bias_grads.reshape(hid)


def solution(mesh):
    placed = (
        P(("row", "col"), None),
        P("row", "col", None, None),
        P("row", "col", None),
        P("row", "col", None, None),
        P("row", "col", None, None, None, None),
        P(),
        P(),
        P(),
        P(("row", "col"), None),
    )
    return jax.shard_map(
        functools.partial(shards, mesh.shape["row"], mesh.shape["col"]),
        mesh=mesh,
        in_specs=placed,
        out_specs=(P(("row", "col"), None), P(("row", "col"), None), P(), P(), P()),
        check_vma=False,
    )
```

```python
import functools

import jax
import jax.numpy as jnp
from jax import lax
from jax.experimental import pallas as pl
from jax.experimental.pallas import tpu as pltpu
from jax.sharding import PartitionSpec as P

BF = jnp.bfloat16
F32 = jnp.float32
MESH = pl.DeviceIdType.MESH
PIECE = 16


def mm(left, right, contract=(1, 0)):
    return lax.dot_general(
        left, right, (((contract[0],), (contract[1],)), ((), ())), preferred_element_type=F32
    )


def each(first, count, body):
    if count - first <= 8:
        for step in sorted(range(first, count), key=lambda s: -min(s, count - s)):
            body(step)
    else:
        lax.fori_loop(first, count, lambda step, carry: (body(step), carry)[1], 0)


def rows_at(ref, index, size):
    if not isinstance(index, int):
        return ref.at[pl.ds(pl.multiple_of(index * size, size), size)]
    return ref.at[pl.ds(index * size, size)]


def layer_kernel(
    row_count, col_count,
    feats_h, rows_h, count_h, tiles_h, values_h, w_self_h, w_neigh_h, bias_h, cot_h,
    hidden_o, base_o, grads_o, bias_o,
    feats, rows, count, tiles, values, w_self, w_neigh, bias, cot,
    feats_t, onehot, outgoing, inbox, weights, weights_t, deg_out, deg_in, part_out, part_in,
    panel, grad_out, grad_in, back_out, back_in,
    piece_out, piece_in,
    load_sem, send_a, recv_a, send_d, recv_d, send_p, recv_p, send_m, recv_m, send_g, recv_g,
    send_t, recv_t, send_c, recv_c, send_x, recv_x, send_y, recv_y, send_z, recv_z,
):
    node_count, in_width = feats.shape
    slot_count = rows.shape[3]
    tile_count = inbox.shape[0] // 128
    depth = tiles.shape[3]
    grad_rows = grads_o.shape[0]
    share = grad_rows // row_count
    piece = max(PIECE, share // col_count)
    owners = share // piece
    total_count = row_count * col_count
    direct = total_count * PIECE == grad_rows
    r = lax.axis_index("row")
    c = lax.axis_index("col")

    def row_peer(step):
        return lax.rem(r + step, row_count)

    def col_peer(step):
        return lax.rem(c + step, col_count)

    me = r * col_count + c

    others = []
    if direct:
        row_peers = [row_peer(step) for step in range(row_count)]
        col_peers = [col_peer(step) for step in range(col_count)]
        for col_step in sorted(range(col_count), key=lambda s: -min(s, col_count - s)):
            for row_step in range(row_count):
                if row_step or col_step:
                    others.append((row_peers[row_step], col_peers[col_step]))

    barrier = pltpu.get_barrier_semaphore()
    if direct:
        for place in others:
            pl.semaphore_signal(barrier, inc=1, device_id=place, device_id_type=MESH)
    else:
        each(1, row_count, lambda s: pl.semaphore_signal(
            barrier, inc=1, device_id=(row_peer(s), c), device_id_type=MESH))
        each(1, col_count, lambda s: pl.semaphore_signal(
            barrier, inc=1, device_id=(r, col_peer(s)), device_id_type=MESH))
    greeted = total_count - 1 if direct else row_count + col_count - 2

    loads = []
    pairs = (
        (rows_h, rows), (count_h, count), (feats_h, feats), (tiles_h, tiles), (values_h, values),
        (w_self_h, w_self), (w_neigh_h, w_neigh), (bias_h, bias), (cot_h, cot),
    )
    for number, (source, target) in enumerate(pairs):
        copy = pltpu.make_async_copy(source, target, load_sem.at[number])
        copy.start()
        loads.append(copy)

    def remote(source, target, send, recv, device):
        return pltpu.make_async_remote_copy(
            src_ref=source, dst_ref=target, send_sem=send, recv_sem=recv,
            device_id=device, device_id_type=MESH)

    def to_row(step, source, target, send, recv, slot=0):
        return remote(source, target, send.at[slot], recv.at[slot], (row_peer(step), c))

    def to_col(step, source, target, send, recv, slot=0):
        return remote(source, target, send.at[slot], recv.at[slot], (r, col_peer(step)))

    def take(ref, length, sem):
        part = ref.at[pl.ds(0, length)]
        pltpu.make_async_copy(part, part, sem.at[0]).wait()

    for copy in loads[:3]:
        copy.wait()
    slot = lax.broadcasted_iota(jnp.int32, (1, slot_count), 1)
    node = lax.broadcasted_iota(jnp.int32, (node_count, slot_count), 0)
    for peer in range(col_count):
        listed = jnp.where(slot < count[0, 0, peer], rows[0, 0, pl.ds(peer, 1), :], -1)
        hot = (node == listed).astype(F32).astype(BF)
        onehot[:, pl.ds(peer * slot_count, slot_count)] = hot
    outgoing[...] = mm(onehot[...], feats[...], (0, 0)).astype(BF)

    pl.semaphore_wait(barrier, greeted)

    def feature_copy(step):
        return to_col(step, rows_at(outgoing, col_peer(step), slot_count),
                      rows_at(inbox, c, slot_count), send_a, recv_a)

    each(1, col_count, lambda s: feature_copy(s).start())
    rows_at(inbox, c, slot_count)[...] = rows_at(outgoing, c, slot_count)[...]

    loads[3].wait()
    loads[4].wait()
    ones = jnp.ones((8, inbox.shape[0]), BF)

    def merge(block):
        for tile in range(tile_count):
            total = jnp.zeros((128, 128), F32)
            for k in range(depth):
                chosen = (tiles[0, 0, block, k] == tile).astype(F32)
                total += values[0, 0, block, k].astype(F32) * chosen
            merged = total.astype(BF)
            rows_at(weights, block, 128)[:, pl.ds(tile * 128, 128)] = merged
        deg_out[block] = mm(ones, rows_at(weights, block, 128)[...], (1, 1))

    each(0, row_count, merge)

    def degree_copy(step):
        return to_row(step, deg_out.at[row_peer(step)], deg_in.at[r], send_d, recv_d)

    each(1, row_count, lambda s: degree_copy(s).start())
    deg_in[r] = deg_out[r]

    def turn(block):
        start = block * 128 if isinstance(block, int) else pl.multiple_of(block * 128, 128)
        weights_t[:, pl.ds(start, 128)] = rows_at(weights, block, 128)[...].astype(F32).T.astype(BF)

    each(0, row_count, turn)
    for copy in loads[5:]:
        copy.wait()
    own_part = mm(feats[...], w_self[...]) + bias[...]
    feats_t[...] = feats[...].astype(F32).T.astype(BF)
    take(deg_in, row_count - 1, recv_d)
    degree = deg_in[0]
    for other in range(1, row_count):
        degree = degree + deg_in[other]
    inverse = 1.0 / jnp.maximum(degree[0:1, :], 1.0)
    inverse = jnp.broadcast_to(inverse, (128, 128)).T

    take(inbox, (col_count - 1) * slot_count, recv_a)

    def partial_copy(step):
        return to_row(step, rows_at(part_out, row_peer(step), 128), part_in.at[r], send_p, recv_p)

    def aggregate(step):
        block = row_peer(step)
        rows_at(part_out, block, 128)[...] = mm(
            rows_at(weights, block, 128)[...], inbox[...]).astype(BF)
        partial_copy(step).start()

    each(1, row_count, aggregate)
    agg_sum = mm(rows_at(weights, r, 128)[...], inbox[...])
    part_in[r] = jnp.zeros((128, in_width), BF)
    take(inbox, (col_count - 1) * slot_count, send_a)
    take(deg_in, row_count - 1, send_d)
    take(part_in, row_count - 1, recv_p)
    for other in range(row_count):
        agg_sum = agg_sum + part_in[other].astype(F32)

    neigh_mean = (agg_sum * inverse).astype(BF)
    preact = own_part + mm(neigh_mean, w_neigh[...])
    sigmoid_pre = jax.nn.sigmoid(preact)
    pre_grads = (
        cot[...].astype(F32) * sigmoid_pre * (1.0 + preact * (1.0 - sigmoid_pre))
    ).astype(BF)
    tile_row = lax.broadcasted_iota(jnp.int32, (PIECE, in_width), 0)

    def pack(first, second):
        value = jnp.where(tile_row % 2 == 0, first, second)
        high = value.astype(BF).astype(F32)
        return jnp.where(tile_row < 2, high, value - high).astype(BF)

    def unpack(packed, length):
        total = packed[0, pl.ds(length, PIECE), :].astype(F32)
        for other in range(1, packed.shape[0]):
            total = total + packed[other, pl.ds(length, PIECE), :].astype(F32)
        return total[0:1] + total[2:3], total[1:2] + total[3:4]

    bias_sum = mm(jnp.ones((8, node_count), BF), pre_grads)
    panel[r, pl.ds(128, PIECE), :] = pack(bias_sum[0:1, :in_width], bias_sum[0:1, in_width:])
    panel[r, pl.ds(0, 128), :] = (mm(pre_grads, w_neigh[...], (1, 1)) * inverse).astype(BF)

    def panel_copy(step):
        return to_row(step, panel.at[r], panel.at[r], send_m, recv_m)

    each(1, row_count, lambda s: panel_copy(s).start())

    half = grad_out.shape[1]
    for number, (left, axis) in enumerate(((feats_t[...], 1), (neigh_mean, 0))):
        product = mm(left, pre_grads, (axis, 0)).astype(BF)
        for side in range(2):
            grad_out[pl.ds((2 * number + side) * in_width, in_width), :] = (
                product[:, side * half:(side + 1) * half])

    def share_copy(step):
        return to_row(step, rows_at(grad_out, row_peer(step), share), grad_in.at[r], send_g, recv_g, step)

    def spread_copy(place):
        owner = place[0] * col_count + place[1]
        return remote(rows_at(grad_out, owner, PIECE), piece_in.at[me],
                      send_c.at[0], recv_c.at[0], place)

    def gather_copy(place):
        own = rows_at(grads_o, me, PIECE)
        return remote(own, own, send_z.at[0], recv_z.at[0], place)

    if direct:
        for place in others:
            spread_copy(place).start()
        piece_in[me] = rows_at(grad_out, me, PIECE)[...]
    else:
        each(1, row_count, lambda s: share_copy(s).start())
        grad_in[r] = rows_at(grad_out, r, share)[...]
    hidden_o[...] = (preact * sigmoid_pre).astype(BF)
    base = mm(pre_grads, w_self[...], (1, 1))

    take(part_in, row_count - 1, send_p)
    take(panel, row_count - 1, recv_m)
    returned = mm(weights_t[:, pl.ds(0, 128)], panel[0, pl.ds(0, 128), :])
    for other in range(1, row_count):
        returned = returned + mm(
            weights_t[:, pl.ds(other * 128, 128)], panel[other, pl.ds(0, 128), :])
    returned = returned.astype(BF)
    bias_tile = pack(*unpack(panel, 128))
    for peer in range(col_count):
        back_out[peer, pl.ds(0, slot_count), :] = returned[peer * slot_count:(peer + 1) * slot_count]
        back_out[peer, pl.ds(slot_count, PIECE), :] = bias_tile

    def back_copy(step):
        return to_col(step, back_out.at[col_peer(step)], back_in.at[c], send_t, recv_t)

    each(1, col_count, lambda s: back_copy(s).start())
    back_in[c] = back_out[c]

    def owning(holder, body):
        if owners == col_count:
            body()
        else:
            pl.when(holder < owners)(body)

    def piece_copy(step):
        return to_col(step, rows_at(piece_out, col_peer(step) % owners, piece),
                      piece_in.at[c], send_c, recv_c, step)

    if direct:
        take(piece_in, total_count - 1, recv_c)
        whole = piece_in[0].astype(F32)
        for other in range(1, total_count):
            whole = whole + piece_in[other].astype(F32)
        rows_at(grads_o, me, PIECE)[...] = whole.astype(BF)
        for place in others:
            gather_copy(place).start()
    else:
        each(1, row_count, lambda s: share_copy(s).wait_recv())
        total = grad_in[0].astype(F32)
        for other in range(1, row_count):
            total = total + grad_in[other].astype(F32)
        piece_out[...] = total.astype(BF)
        each(1, col_count, lambda s: owning(col_peer(s), lambda: piece_copy(s).start()))
        piece_in[c] = rows_at(piece_out, c % owners, piece)[...]

    def final_piece(holder):
        start = r * share + holder * piece
        return grads_o.at[pl.ds(pl.multiple_of(start, piece), piece)]

    def final_copy(step):
        return to_col(step, final_piece(c), final_piece(c), send_x, recv_x, step)

    def reduce_piece():
        each(1, col_count, lambda s: piece_copy(s).wait_recv())
        whole = piece_in[0].astype(F32)
        for other in range(1, col_count):
            whole = whole + piece_in[other].astype(F32)
        final_piece(c)[...] = whole.astype(BF)
        each(1, col_count, lambda s: final_copy(s).start())

    if not direct:
        owning(c, reduce_piece)

    take(back_in, col_count - 1, recv_t)
    arrived = jnp.concatenate(
        [back_in[peer, pl.ds(0, slot_count), :] for peer in range(col_count)], axis=0)
    base_o[...] = base + mm(onehot[...], arrived)
    bias_o[...] = jnp.broadcast_to(
        jnp.concatenate(unpack(back_in, slot_count), axis=1), bias_o.shape)
    take(panel, row_count - 1, send_m)
    take(back_in, col_count - 1, send_t)

    def share_final(step):
        own = rows_at(grads_o, r, share)
        return to_row(step, own, own, send_y, recv_y, step)

    if direct:
        take(piece_in, total_count - 1, send_c)
        take(grads_o, (total_count - 1) * PIECE, send_z)
        take(grads_o, (total_count - 1) * PIECE, recv_z)
    else:
        each(1, col_count, lambda s: owning(lax.rem(c + col_count - s, col_count), lambda: final_copy(s).wait_recv()))
        each(1, row_count, lambda s: share_final(s).start())
        each(1, row_count, lambda s: share_final(s).wait_recv())
        for step_copy in (share_copy, share_final):
            each(1, row_count, lambda s: step_copy(s).wait_send())
        each(1, col_count, lambda s: owning(col_peer(s), lambda: piece_copy(s).wait_send()))
        owning(c, lambda: each(1, col_count, lambda s: final_copy(s).wait_send()))


def write_kernel(hidden_i, base_i, grads_i, bias_i, hidden, base, self_grads, neigh_grads, bias):
    hidden[...] = hidden_i[...]
    base[...] = base_i[...]
    rows, width = self_grads.shape
    half = grads_i.shape[1]
    for number, target in enumerate((self_grads, neigh_grads)):
        for side in range(width // half):
            block = grads_i[pl.ds((2 * number + side) * rows, rows), :]
            target[:, pl.ds(side * half, half)] = block.astype(F32)
    bias[...] = bias_i[0:1, :]


def shards(row_count, col_count, node_feats, send_rows, send_count, block_tiles, block_values,
           w_self, w_neigh, bias_term, cotangent):
    nodes, width = node_feats.shape
    hid = w_self.shape[1]
    half = hid // 2
    slots = send_rows.shape[3]
    received = col_count * slots
    panel = row_count * nodes
    grad_rows = 4 * width
    share = grad_rows // row_count
    piece = max(PIECE, share // col_count)
    total = row_count * col_count
    pieces = total if total * PIECE == grad_rows else col_count
    piece_sems = pltpu.SemaphoreType.DMA((pieces,))
    bias_term = bias_term.reshape(1, hid)
    arrays = (node_feats, send_rows, send_count, block_tiles, block_values, w_self, w_neigh,
              bias_term, cotangent)
    spaces = (pltpu.VMEM, pltpu.VMEM, pltpu.SMEM, pltpu.SMEM) + (pltpu.VMEM,) * 5
    row_sems = pltpu.SemaphoreType.DMA((row_count,))
    col_sems = pltpu.SemaphoreType.DMA((col_count,))
    vmem = pl.BlockSpec(memory_space=pltpu.VMEM)
    scratch = [space(array.shape, array.dtype) for space, array in zip(spaces, arrays)] + [
        pltpu.VMEM((width, nodes), BF),
        pltpu.VMEM((nodes, received), BF),
        pltpu.VMEM((received, width), BF),
        pltpu.VMEM((received, width), BF),
        pltpu.VMEM((panel, received), BF),
        pltpu.VMEM((received, panel), BF),
        pltpu.VMEM((row_count, 8, nodes), F32),
        pltpu.VMEM((row_count, 8, nodes), F32),
        pltpu.VMEM((panel, width), BF),
        pltpu.VMEM((row_count, nodes, width), BF),
        pltpu.VMEM((row_count, nodes + PIECE, width), BF),
        pltpu.VMEM((grad_rows, half), BF),
        pltpu.VMEM((row_count, share, half), BF),
        pltpu.VMEM((col_count, slots + PIECE, width), BF),
        pltpu.VMEM((col_count, slots + PIECE, width), BF),
        pltpu.VMEM((share, half), BF),
        pltpu.VMEM((pieces, piece, half), BF),
        pltpu.SemaphoreType.DMA((len(arrays),)),
        col_sems, col_sems, row_sems, row_sems, row_sems, row_sems, row_sems, row_sems,
        row_sems, row_sems, col_sems, col_sems, piece_sems, piece_sems,
        col_sems, col_sems, row_sems, row_sems, piece_sems, piece_sems,
    ]
    results = pl.pallas_call(
        functools.partial(layer_kernel, row_count, col_count),
        out_shape=(
            jax.ShapeDtypeStruct((nodes, hid), BF),
            jax.ShapeDtypeStruct((nodes, width), F32),
            jax.ShapeDtypeStruct((grad_rows, half), BF),
            jax.ShapeDtypeStruct((8, hid), F32),
        ),
        in_specs=[pl.BlockSpec(memory_space=pltpu.HBM)] * len(arrays),
        out_specs=(vmem,) * 4,
        scratch_shapes=scratch,
        compiler_params=pltpu.CompilerParams(
            collective_id=0, has_side_effects=True, vmem_limit_bytes=40 * 1024 * 1024),
    )(*[pltpu.with_memory_space_constraint(a, pltpu.HBM) for a in arrays])
    hidden, input_grads, self_grads, neigh_grads, bias_grads = pl.pallas_call(
        write_kernel,
        out_shape=(
            jax.ShapeDtypeStruct((nodes, hid), BF),
            jax.ShapeDtypeStruct((nodes, width), F32),
            jax.ShapeDtypeStruct((width, hid), F32),
            jax.ShapeDtypeStruct((width, hid), F32),
            jax.ShapeDtypeStruct((1, hid), F32),
        ),
        in_specs=[vmem] * 4,
        out_specs=(vmem,) * 5,
        compiler_params=pltpu.CompilerParams(vmem_limit_bytes=4 * 1024 * 1024),
    )(*results)
    return hidden, input_grads, self_grads, neigh_grads, bias_grads.reshape(hid)


def solution(mesh):
    placed = (
        P(("row", "col"), None),
        P("row", "col", None, None),
        P("row", "col", None),
        P("row", "col", None, None),
        P("row", "col", None, None, None, None),
        P(),
        P(),
        P(),
        P(("row", "col"), None),
    )
    return jax.shard_map(
        functools.partial(shards, mesh.shape["row"], mesh.shape["col"]),
        mesh=mesh,
        in_specs=placed,
        out_specs=(P(("row", "col"), None), P(("row", "col"), None), P(), P(), P()),
        check_vma=False,
    )
```

```python
import functools

import jax
import jax.numpy as jnp
from jax import lax
from jax.experimental import pallas as pl
from jax.experimental.pallas import tpu as pltpu
from jax.sharding import PartitionSpec as P

BF = jnp.bfloat16
F32 = jnp.float32
MESH = pl.DeviceIdType.MESH
PIECE = 16


def mm(left, right, contract=(1, 0)):
    return lax.dot_general(
        left, right, (((contract[0],), (contract[1],)), ((), ())), preferred_element_type=F32
    )


def each(first, count, body):
    if count - first <= 8:
        for step in sorted(range(first, count), key=lambda s: -min(s, count - s)):
            body(step)
    else:
        lax.fori_loop(first, count, lambda step, carry: (body(step), carry)[1], 0)


def rows_at(ref, index, size):
    if not isinstance(index, int):
        return ref.at[pl.ds(pl.multiple_of(index * size, size), size)]
    return ref.at[pl.ds(index * size, size)]


def layer_kernel(
    row_count, col_count,
    feats_h, rows_h, count_h, tiles_h, values_h, w_self_h, w_neigh_h, bias_h, cot_h,
    hidden_o, base_o, grads_o, bias_o,
    feats, rows, count, tiles, values, w_self, w_neigh, bias, cot,
    feats_t, onehot, outgoing, inbox, weights, weights_t, deg_out, deg_in, part_out, part_in,
    panel, grad_out, grad_in, back_out, back_in,
    piece_out, piece_in,
    load_sem, send_a, recv_a, send_d, recv_d, send_p, recv_p, send_m, recv_m, send_g, recv_g,
    send_t, recv_t, send_c, recv_c, send_x, recv_x, send_y, recv_y, send_z, recv_z,
):
    node_count, in_width = feats.shape
    slot_count = rows.shape[3]
    tile_count = inbox.shape[0] // 128
    depth = tiles.shape[3]
    grad_rows = grads_o.shape[0]
    share = grad_rows // row_count
    piece = max(PIECE, share // col_count)
    owners = share // piece
    total_count = row_count * col_count
    direct = total_count * PIECE == grad_rows
    r = lax.axis_index("row")
    c = lax.axis_index("col")

    def row_peer(step):
        return lax.rem(r + step, row_count)

    def col_peer(step):
        return lax.rem(c + step, col_count)

    me = r * col_count + c

    others = []
    if direct:
        row_peers = [row_peer(step) for step in range(row_count)]
        col_peers = [col_peer(step) for step in range(col_count)]
        for col_step in range(col_count):
            for row_step in range(row_count):
                if row_step or col_step:
                    others.append((row_peers[row_step], col_peers[col_step]))

    barrier = pltpu.get_barrier_semaphore()
    if direct:
        for place in others:
            pl.semaphore_signal(barrier, inc=1, device_id=place, device_id_type=MESH)
    else:
        each(1, row_count, lambda s: pl.semaphore_signal(
            barrier, inc=1, device_id=(row_peer(s), c), device_id_type=MESH))
        each(1, col_count, lambda s: pl.semaphore_signal(
            barrier, inc=1, device_id=(r, col_peer(s)), device_id_type=MESH))
    greeted = total_count - 1 if direct else row_count + col_count - 2

    loads = []
    pairs = (
        (rows_h, rows), (count_h, count), (feats_h, feats), (tiles_h, tiles), (values_h, values),
        (w_self_h, w_self), (w_neigh_h, w_neigh), (bias_h, bias), (cot_h, cot),
    )
    for number, (source, target) in enumerate(pairs):
        copy = pltpu.make_async_copy(source, target, load_sem.at[number])
        copy.start()
        loads.append(copy)

    def remote(source, target, send, recv, device):
        return pltpu.make_async_remote_copy(
            src_ref=source, dst_ref=target, send_sem=send, recv_sem=recv,
            device_id=device, device_id_type=MESH)

    def to_row(step, source, target, send, recv, slot=0):
        return remote(source, target, send.at[slot], recv.at[slot], (row_peer(step), c))

    def to_col(step, source, target, send, recv, slot=0):
        return remote(source, target, send.at[slot], recv.at[slot], (r, col_peer(step)))

    def take(ref, length, sem):
        part = ref.at[pl.ds(0, length)]
        pltpu.make_async_copy(part, part, sem.at[0]).wait()

    for copy in loads[:3]:
        copy.wait()
    slot = lax.broadcasted_iota(jnp.int32, (1, slot_count), 1)
    node = lax.broadcasted_iota(jnp.int32, (node_count, slot_count), 0)
    for peer in range(col_count):
        listed = jnp.where(slot < count[0, 0, peer], rows[0, 0, pl.ds(peer, 1), :], -1)
        hot = (node == listed).astype(F32).astype(BF)
        onehot[:, pl.ds(peer * slot_count, slot_count)] = hot
    outgoing[...] = mm(onehot[...], feats[...], (0, 0)).astype(BF)

    pl.semaphore_wait(barrier, greeted)

    def feature_copy(step):
        return to_col(step, rows_at(outgoing, col_peer(step), slot_count),
                      rows_at(inbox, c, slot_count), send_a, recv_a)

    each(1, col_count, lambda s: feature_copy(s).start())
    rows_at(inbox, c, slot_count)[...] = rows_at(outgoing, c, slot_count)[...]

    loads[3].wait()
    loads[4].wait()
    ones = jnp.ones((8, inbox.shape[0]), BF)

    def merge(block):
        for tile in range(tile_count):
            total = jnp.zeros((128, 128), F32)
            for k in range(depth):
                chosen = (tiles[0, 0, block, k] == tile).astype(F32)
                total += values[0, 0, block, k].astype(F32) * chosen
            merged = total.astype(BF)
            rows_at(weights, block, 128)[:, pl.ds(tile * 128, 128)] = merged
        deg_out[block] = mm(ones, rows_at(weights, block, 128)[...], (1, 1))

    each(0, row_count, merge)

    def degree_copy(step):
        return to_row(step, deg_out.at[row_peer(step)], deg_in.at[r], send_d, recv_d)

    each(1, row_count, lambda s: degree_copy(s).start())
    deg_in[r] = deg_out[r]

    def turn(block):
        start = block * 128 if isinstance(block, int) else pl.multiple_of(block * 128, 128)
        weights_t[:, pl.ds(start, 128)] = rows_at(weights, block, 128)[...].astype(F32).T.astype(BF)

    each(0, row_count, turn)
    for copy in loads[5:]:
        copy.wait()
    own_part = mm(feats[...], w_self[...]) + bias[...]
    feats_t[...] = feats[...].astype(F32).T.astype(BF)
    take(deg_in, row_count - 1, recv_d)
    degree = deg_in[0]
    for other in range(1, row_count):
        degree = degree + deg_in[other]
    inverse = 1.0 / jnp.maximum(degree[0:1, :], 1.0)
    inverse = jnp.broadcast_to(inverse, (128, 128)).T

    take(inbox, (col_count - 1) * slot_count, recv_a)

    def partial_copy(step):
        return to_row(step, rows_at(part_out, row_peer(step), 128), part_in.at[r], send_p, recv_p)

    def aggregate(step):
        block = row_peer(step)
        rows_at(part_out, block, 128)[...] = mm(
            rows_at(weights, block, 128)[...], inbox[...]).astype(BF)
        partial_copy(step).start()

    each(1, row_count, aggregate)
    agg_sum = mm(rows_at(weights, r, 128)[...], inbox[...])
    part_in[r] = jnp.zeros((128, in_width), BF)
    take(inbox, (col_count - 1) * slot_count, send_a)
    take(deg_in, row_count - 1, send_d)
    take(part_in, row_count - 1, recv_p)
    for other in range(row_count):
        agg_sum = agg_sum + part_in[other].astype(F32)

    neigh_mean = (agg_sum * inverse).astype(BF)
    preact = own_part + mm(neigh_mean, w_neigh[...])
    sigmoid_pre = jax.nn.sigmoid(preact)
    pre_grads = (
        cot[...].astype(F32) * sigmoid_pre * (1.0 + preact * (1.0 - sigmoid_pre))
    ).astype(BF)
    tile_row = lax.broadcasted_iota(jnp.int32, (PIECE, in_width), 0)

    def pack(first, second):
        value = jnp.where(tile_row % 2 == 0, first, second)
        high = value.astype(BF).astype(F32)
        return jnp.where(tile_row < 2, high, value - high).astype(BF)

    def unpack(packed, length):
        total = packed[0, pl.ds(length, PIECE), :].astype(F32)
        for other in range(1, packed.shape[0]):
            total = total + packed[other, pl.ds(length, PIECE), :].astype(F32)
        return total[0:1] + total[2:3], total[1:2] + total[3:4]

    bias_sum = mm(jnp.ones((8, node_count), BF), pre_grads)
    panel[r, pl.ds(128, PIECE), :] = pack(bias_sum[0:1, :in_width], bias_sum[0:1, in_width:])
    panel[r, pl.ds(0, 128), :] = (mm(pre_grads, w_neigh[...], (1, 1)) * inverse).astype(BF)

    def panel_copy(step):
        return to_row(step, panel.at[r], panel.at[r], send_m, recv_m)

    each(1, row_count, lambda s: panel_copy(s).start())

    half = grad_out.shape[1]
    for number, (left, axis) in enumerate(((feats_t[...], 1), (neigh_mean, 0))):
        product = mm(left, pre_grads, (axis, 0)).astype(BF)
        for side in range(2):
            grad_out[pl.ds((2 * number + side) * in_width, in_width), :] = (
                product[:, side * half:(side + 1) * half])

    def share_copy(step):
        return to_row(step, rows_at(grad_out, row_peer(step), share), grad_in.at[r], send_g, recv_g, step)

    def spread_copy(place):
        owner = place[0] * col_count + place[1]
        return remote(rows_at(grad_out, owner, PIECE), piece_in.at[me],
                      send_c.at[0], recv_c.at[0], place)

    def gather_copy(place):
        own = rows_at(grads_o, me, PIECE)
        return remote(own, own, send_z.at[0], recv_z.at[0], place)

    if direct:
        for place in others:
            spread_copy(place).start()
        piece_in[me] = rows_at(grad_out, me, PIECE)[...]
    else:
        each(1, row_count, lambda s: share_copy(s).start())
        grad_in[r] = rows_at(grad_out, r, share)[...]
    base = mm(pre_grads, w_self[...], (1, 1))

    take(part_in, row_count - 1, send_p)
    take(panel, row_count - 1, recv_m)
    returned = mm(weights_t[:, pl.ds(0, 128)], panel[0, pl.ds(0, 128), :])
    for other in range(1, row_count):
        returned = returned + mm(
            weights_t[:, pl.ds(other * 128, 128)], panel[other, pl.ds(0, 128), :])
    returned = returned.astype(BF)
    bias_tile = pack(*unpack(panel, 128))
    for peer in range(col_count):
        back_out[peer, pl.ds(0, slot_count), :] = returned[peer * slot_count:(peer + 1) * slot_count]
        back_out[peer, pl.ds(slot_count, PIECE), :] = bias_tile

    def back_copy(step):
        return to_col(step, back_out.at[col_peer(step)], back_in.at[c], send_t, recv_t)

    each(1, col_count, lambda s: back_copy(s).start())
    back_in[c] = back_out[c]

    def owning(holder, body):
        if owners == col_count:
            body()
        else:
            pl.when(holder < owners)(body)

    def piece_copy(step):
        return to_col(step, rows_at(piece_out, col_peer(step) % owners, piece),
                      piece_in.at[c], send_c, recv_c, step)

    if direct:
        take(piece_in, total_count - 1, recv_c)
        whole = piece_in[0].astype(F32)
        for other in range(1, total_count):
            whole = whole + piece_in[other].astype(F32)
        rows_at(grads_o, me, PIECE)[...] = whole.astype(BF)
        for place in others:
            gather_copy(place).start()
    else:
        each(1, row_count, lambda s: share_copy(s).wait_recv())
        total = grad_in[0].astype(F32)
        for other in range(1, row_count):
            total = total + grad_in[other].astype(F32)
        piece_out[...] = total.astype(BF)
        each(1, col_count, lambda s: owning(col_peer(s), lambda: piece_copy(s).start()))
        piece_in[c] = rows_at(piece_out, c % owners, piece)[...]

    def final_piece(holder):
        start = r * share + holder * piece
        return grads_o.at[pl.ds(pl.multiple_of(start, piece), piece)]

    def final_copy(step):
        return to_col(step, final_piece(c), final_piece(c), send_x, recv_x, step)

    def reduce_piece():
        each(1, col_count, lambda s: piece_copy(s).wait_recv())
        whole = piece_in[0].astype(F32)
        for other in range(1, col_count):
            whole = whole + piece_in[other].astype(F32)
        final_piece(c)[...] = whole.astype(BF)
        each(1, col_count, lambda s: final_copy(s).start())

    if not direct:
        owning(c, reduce_piece)

    take(back_in, col_count - 1, recv_t)
    arrived = jnp.concatenate(
        [back_in[peer, pl.ds(0, slot_count), :] for peer in range(col_count)], axis=0)
    base_o[...] = base + mm(onehot[...], arrived)
    bias_o[...] = jnp.broadcast_to(
        jnp.concatenate(unpack(back_in, slot_count), axis=1), bias_o.shape)
    hidden_o[...] = (preact * sigmoid_pre).astype(BF)
    take(panel, row_count - 1, send_m)
    take(back_in, col_count - 1, send_t)

    def share_final(step):
        own = rows_at(grads_o, r, share)
        return to_row(step, own, own, send_y, recv_y, step)

    if direct:
        take(piece_in, total_count - 1, send_c)
        take(grads_o, (total_count - 1) * PIECE, send_z)
        take(grads_o, (total_count - 1) * PIECE, recv_z)
    else:
        each(1, col_count, lambda s: owning(lax.rem(c + col_count - s, col_count), lambda: final_copy(s).wait_recv()))
        each(1, row_count, lambda s: share_final(s).start())
        each(1, row_count, lambda s: share_final(s).wait_recv())
        for step_copy in (share_copy, share_final):
            each(1, row_count, lambda s: step_copy(s).wait_send())
        each(1, col_count, lambda s: owning(col_peer(s), lambda: piece_copy(s).wait_send()))
        owning(c, lambda: each(1, col_count, lambda s: final_copy(s).wait_send()))


def write_kernel(hidden_i, base_i, grads_i, bias_i, hidden, base, self_grads, neigh_grads, bias):
    hidden[...] = hidden_i[...]
    base[...] = base_i[...]
    rows, width = self_grads.shape
    half = grads_i.shape[1]
    for number, target in enumerate((self_grads, neigh_grads)):
        for side in range(width // half):
            block = grads_i[pl.ds((2 * number + side) * rows, rows), :]
            target[:, pl.ds(side * half, half)] = block.astype(F32)
    bias[...] = bias_i[0:1, :]


def shards(row_count, col_count, node_feats, send_rows, send_count, block_tiles, block_values,
           w_self, w_neigh, bias_term, cotangent):
    nodes, width = node_feats.shape
    hid = w_self.shape[1]
    half = hid // 2
    slots = send_rows.shape[3]
    received = col_count * slots
    panel = row_count * nodes
    grad_rows = 4 * width
    share = grad_rows // row_count
    piece = max(PIECE, share // col_count)
    total = row_count * col_count
    pieces = total if total * PIECE == grad_rows else col_count
    piece_sems = pltpu.SemaphoreType.DMA((pieces,))
    bias_term = bias_term.reshape(1, hid)
    arrays = (node_feats, send_rows, send_count, block_tiles, block_values, w_self, w_neigh,
              bias_term, cotangent)
    spaces = (pltpu.VMEM, pltpu.VMEM, pltpu.SMEM, pltpu.SMEM) + (pltpu.VMEM,) * 5
    row_sems = pltpu.SemaphoreType.DMA((row_count,))
    col_sems = pltpu.SemaphoreType.DMA((col_count,))
    vmem = pl.BlockSpec(memory_space=pltpu.VMEM)
    scratch = [space(array.shape, array.dtype) for space, array in zip(spaces, arrays)] + [
        pltpu.VMEM((width, nodes), BF),
        pltpu.VMEM((nodes, received), BF),
        pltpu.VMEM((received, width), BF),
        pltpu.VMEM((received, width), BF),
        pltpu.VMEM((panel, received), BF),
        pltpu.VMEM((received, panel), BF),
        pltpu.VMEM((row_count, 8, nodes), F32),
        pltpu.VMEM((row_count, 8, nodes), F32),
        pltpu.VMEM((panel, width), BF),
        pltpu.VMEM((row_count, nodes, width), BF),
        pltpu.VMEM((row_count, nodes + PIECE, width), BF),
        pltpu.VMEM((grad_rows, half), BF),
        pltpu.VMEM((row_count, share, half), BF),
        pltpu.VMEM((col_count, slots + PIECE, width), BF),
        pltpu.VMEM((col_count, slots + PIECE, width), BF),
        pltpu.VMEM((share, half), BF),
        pltpu.VMEM((pieces, piece, half), BF),
        pltpu.SemaphoreType.DMA((len(arrays),)),
        col_sems, col_sems, row_sems, row_sems, row_sems, row_sems, row_sems, row_sems,
        row_sems, row_sems, col_sems, col_sems, piece_sems, piece_sems,
        col_sems, col_sems, row_sems, row_sems, piece_sems, piece_sems,
    ]
    results = pl.pallas_call(
        functools.partial(layer_kernel, row_count, col_count),
        out_shape=(
            jax.ShapeDtypeStruct((nodes, hid), BF),
            jax.ShapeDtypeStruct((nodes, width), F32),
            jax.ShapeDtypeStruct((grad_rows, half), BF),
            jax.ShapeDtypeStruct((8, hid), F32),
        ),
        in_specs=[pl.BlockSpec(memory_space=pltpu.HBM)] * len(arrays),
        out_specs=(vmem,) * 4,
        scratch_shapes=scratch,
        compiler_params=pltpu.CompilerParams(
            collective_id=0, has_side_effects=True, vmem_limit_bytes=40 * 1024 * 1024),
    )(*[pltpu.with_memory_space_constraint(a, pltpu.HBM) for a in arrays])
    hidden, input_grads, self_grads, neigh_grads, bias_grads = pl.pallas_call(
        write_kernel,
        out_shape=(
            jax.ShapeDtypeStruct((nodes, hid), BF),
            jax.ShapeDtypeStruct((nodes, width), F32),
            jax.ShapeDtypeStruct((width, hid), F32),
            jax.ShapeDtypeStruct((width, hid), F32),
            jax.ShapeDtypeStruct((1, hid), F32),
        ),
        in_specs=[vmem] * 4,
        out_specs=(vmem,) * 5,
        compiler_params=pltpu.CompilerParams(vmem_limit_bytes=4 * 1024 * 1024),
    )(*results)
    return hidden, input_grads, self_grads, neigh_grads, bias_grads.reshape(hid)


def solution(mesh):
    placed = (
        P(("row", "col"), None),
        P("row", "col", None, None),
        P("row", "col", None),
        P("row", "col", None, None),
        P("row", "col", None, None, None, None),
        P(),
        P(),
        P(),
        P(("row", "col"), None),
    )
    return jax.shard_map(
        functools.partial(shards, mesh.shape["row"], mesh.shape["col"]),
        mesh=mesh,
        in_specs=placed,
        out_specs=(P(("row", "col"), None), P(("row", "col"), None), P(), P(), P()),
        check_vma=False,
    )
```
